128 devices in a mesh: chan: 64 (over x, z_hi, y, core), win: 2 (over z_lo).
Axes of the slice: x: 4, y: 4, z: 4 (z_hi: 2, z_lo: 2; z = z_hi * 2 + z_lo), core: 2. Of those that a mesh axis runs over, the one named last changes fastest.
Arguments:
- spectra: bfloat16 [2, 256, 64, 8192], P(None, None, 'win', 'chan'), may hold values from -6 to 6
- freq_idx: int32 [64], replicated, may hold values from 0 to 255
- pairing: int32 [6, 64], replicated, may hold values from 0 to 63, as said below
Outputs:
- crossspec: bfloat16 [2, 6, 64, 8192, 128], P(None, None, 'win', 'chan')
The draws below stay inside these ranges and needn't reach their ends.
Inputs may be any that keep to these rules, and one draw needn't show every extreme that they name: Each row pairs the 64 blocks two by two: pairing[r, pairing[r, b]] = b and pairing[r, b] != b.
All inputs are finite; a program needn't handle non-finite values.
Results may differ from the reference program's by a relative error of at most 0.012.
Values may be sent and summed in bfloat16 or wider, within the bound.
A program may use at most 192 MiB of HBM per device.

```python
import math
import jax
import jax.numpy as jnp
from jax import lax

CB = 128
NBINS = 256
F = 64
ROUNDS = 6
W_DEV = 32
CH = 8192
WINDOWS = 64
N_CHAN = 64
N_WIN = 2


def draw_pairing(key, part):
    key = jax.random.fold_in(key, 7)
    keys = jax.random.split(key, ROUNDS)

    def one_round(round_key):
        order = jax.random.permutation(round_key, N_CHAN).astype(jnp.int32)
        inverse = jnp.argsort(order).astype(jnp.int32)
        mate_pos = inverse + 1 - 2 * (inverse % 2)
        return order[mate_pos].astype(jnp.int32)
    return jax.vmap(one_round)(keys)


def place_ends(result, own_key, smallest, high):
    dims = result.shape
    index_at = [jax.random.randint(jax.random.fold_in(own_key, axis), (), 0, dims[axis]) for axis in range(len(dims))]
    result = result.at[tuple(index_at)].set(smallest)
    longest = dims.index(max(dims))
    index_at[longest] = (index_at[longest] + 1) % dims[longest]
    return result.at[tuple(index_at)].set(high)


def shard_levels(key, extent, shards, least, top_value):
    def one(dim, blocks):
        steps = jax.random.uniform(jax.random.fold_in(jax.random.fold_in(key, 6), dim), (blocks,), jnp.float32, least / len(shards), top_value / len(shards))
        return jnp.repeat(jnp.exp(steps), extent[dim] // blocks).reshape((-1,) + (1,) * (len(extent) - dim - 1))

    level = one(*shards[0])
    for cut in shards[1:]:
        level = level * one(*cut)
    return level


def noise(own_key, extent, spread, bound, cuts=(), kind=jnp.bfloat16):
    factor_of = shard_levels(own_key, extent, cuts, -0.22, 0.18) if cuts else 1.0
    array = jax.random.normal(own_key, extent, jnp.float32) * spread * factor_of
    return jnp.minimum(jnp.maximum(array, -bound), bound).astype(kind)


def setup_inputs(seed: int = 0) -> dict:
    key_list = jax.random.split(jax.random.key(seed), 4)
    spectra = noise(key_list[0], (2, NBINS, WINDOWS, CH), 1.0, 6.0, ((2, 2), (3, 64)))
    freq_idx = place_ends(jax.random.randint(key_list[1], (F,), 0, NBINS), jax.random.fold_in(key_list[1], 1), 0, NBINS - 1).astype(jnp.int32)
    pairing = draw_pairing(jax.random.fold_in(key_list[3], 71), 0)
    return dict(spectra=spectra, freq_idx=freq_idx, pairing=pairing)


def pair_products(left, right):
    return jnp.einsum('gwbi,gwbj->gbij', left, right, precision=lax.Precision.HIGHEST)

def reference(spectra, freq_idx, pairing):
    selected = jnp.take(spectra, freq_idx, axis=1)
    scale = 1.0 / math.sqrt(WINDOWS)

    def one_bin(values):
        blocks = values.reshape(2, N_WIN, W_DEV, N_CHAN, CB).astype(jnp.float32)
        results = []
        for step in range(ROUNDS):
            partner = jnp.take(blocks, pairing[step], axis=3)
            real_part = pair_products(blocks[0], partner[0]) + pair_products(blocks[1], partner[1])
            imag_part = pair_products(blocks[1], partner[0]) - pair_products(blocks[0], partner[1])
            partial_value = (jnp.stack([real_part, imag_part]) * scale).astype(jnp.bfloat16)
            total = lax.optimization_barrier(jnp.sum(partial_value.astype(jnp.float32), axis=1))
            results.append(total.reshape(2, N_CHAN * CB, CB))
        return jnp.stack(results, 1)
    stacked = lax.map(one_bin, jnp.moveaxis(selected, 1, 0))
    return jnp.transpose(stacked, (1, 2, 0, 3, 4)).astype(jnp.bfloat16)
```

```python
import functools
import math

import jax
import jax.numpy as jnp
from jax import lax
from jax.experimental import pallas as pl
from jax.experimental.pallas import tpu as pltpu
from jax.sharding import PartitionSpec as P


def pair_kernel(scale, own_ref, part_ref, out_ref):
    rounds = part_ref.shape[2]
    channels = own_ref.shape[3]
    for b in range(own_ref.shape[1]):
        real, imag = own_ref[0, b], own_ref[1, b]
        left = jnp.concatenate(
            [jnp.concatenate([real, imag], 0).T, jnp.concatenate([imag, -real], 0).T], 0
        )
        for r in range(0, rounds, 2):
            right = jnp.concatenate(
                [
                    jnp.concatenate([part_ref[b, 0, q], part_ref[b, 1, q]], 0)
                    for q in (r, r + 1)
                ],
                1,
            )
            product = jnp.dot(left, right, preferred_element_type=jnp.float32) * scale
            product = product.astype(out_ref.dtype)
            for half in range(2):
                for q in range(2):
                    out_ref[half, r + q, b] = product[
                        half * channels : (half + 1) * channels,
                        q * channels : (q + 1) * channels,
                    ]


def pair_products(own, part, scale):
    bins, _, rounds, windows, channels = part.shape
    step = 2
    return pl.pallas_call(
        functools.partial(pair_kernel, scale),
        grid=(bins // step,),
        out_shape=jax.ShapeDtypeStruct((2, rounds, bins, channels, channels), own.dtype),
        in_specs=[
            pl.BlockSpec((2, step, windows, channels), lambda i: (0, i, 0, 0)),
            pl.BlockSpec((step, 2, rounds, windows, channels), lambda i: (i, 0, 0, 0, 0)),
        ],
        out_specs=pl.BlockSpec((2, rounds, step, channels, channels), lambda i: (0, 0, i, 0, 0)),
        compiler_params=pltpu.CompilerParams(vmem_limit_bytes=32 << 20),
        name="pair_products",
    )(own, part)


def body(spectra, freq_idx, pairing):
    nblocks = lax.axis_size("chan")
    nwin = lax.axis_size("win")
    rounds = pairing.shape[0]
    selected = jnp.take(spectra, freq_idx, axis=1)
    _, fbins, width, channels = selected.shape
    scale = 1.0 / math.sqrt(width * nwin)
    own = lax.all_to_all(selected, "win", split_axis=1, concat_axis=2, tiled=True)
    units = jnp.transpose(selected, (1, 0, 2, 3)).reshape(fbins * 2, width, channels)
    spread = lax.all_to_all(units, ("win", "chan"), split_axis=0, concat_axis=0, tiled=True)
    blocks = jnp.transpose(spread.reshape(nwin, nblocks, width, channels), (1, 0, 2, 3))
    wanted = jnp.take(blocks.reshape(nblocks, nwin * width, channels), pairing.T, axis=0)
    part = lax.all_to_all(wanted, "chan", split_axis=0, concat_axis=0, tiled=True)
    part = part.reshape(fbins // nwin, 2, rounds, nwin * width, channels)
    return pair_products(own, part, scale)


def solution(mesh):
    return jax.shard_map(
        body,
        mesh=mesh,
        in_specs=(P(None, None, "win", "chan"), P(), P()),
        out_specs=P(None, None, "win", "chan", None),
        check_vma=False,
    )
```

```python
import functools
import math

import jax
import jax.numpy as jnp
from jax import lax
from jax.experimental import pallas as pl
from jax.experimental.pallas import tpu as pltpu
from jax.sharding import PartitionSpec as P

MESH = pl.DeviceIdType.MESH


def block_of(x, zh, y, c):
    return ((x * 2 + zh) * 4 + y) * 2 + c


def place(x, zh, w, y, c):
    return {"chan": block_of(x, zh, y, c), "win": w}


def move_kernel(
    spectra, freq, pairing, part, own,
    whole, sel, held_a, held_b, half_c, held_c, stage,
    load_sem, spread_send, spread_recv, ring_send, ring_recv,
    own_send, own_recv, part_send, part_recv,
):
    chan = lax.axis_index("chan")
    w = lax.axis_index("win")
    c = chan % 2
    y = (chan // 2) % 4
    zh = (chan // 8) % 2
    x = chan // 16
    rounds = pairing.shape[0]

    load = pltpu.make_async_copy(spectra, whole, load_sem)
    load.start()

    barrier = pltpu.get_barrier_semaphore()

    def greet(dx, dz, dy, dc):
        z = (zh * 2 + w + dz) % 4
        pl.semaphore_signal(
            barrier, inc=1, device_id=place((x + dx) % 4, z // 2, z % 2, (y + dy) % 4, (c + dc) % 2),
            device_id_type=MESH,
        )

    def greet_plane(o, carry):
        dc, one, two = o % 2, (o // 2) % 4, o // 8
        greet(0, one, two, dc)

        @pl.when(two > 0)
        def _():
            greet(two, one, 0, dc)

        @pl.when((one > 0) & (two > 0))
        def _():
            greet(one, 0, two, dc)

        return carry

    lax.fori_loop(1, 32, greet_plane, 0)
    load.wait()

    def pick(k, carry):
        f = freq[k]
        for part_index in range(2):
            sel[part_index, k // 32, k % 32] = whole[part_index, f]
        return carry

    lax.fori_loop(0, 64, pick, 0)
    pl.semaphore_wait(barrier, 31 + 24 + 18)

    def send(src, dst, ssem, rsem, target):
        pltpu.make_async_remote_copy(
            src_ref=src, dst_ref=dst, send_sem=ssem, recv_sem=rsem, device_id=target, device_id_type=MESH
        ).start()

    mine_a = block_of(x, zh, y, c)
    mine_b = y * 16 + (x * 2 + zh) * 2 + c
    mine_c = (x * 4 + y) * 2 + c

    def src_a(zh2, w2, y2):
        return sel.at[zh2, w2, pl.ds(2 * y2, 2)]

    def src_b(zh2, w2, x2):
        return sel.at[zh2, w2, pl.ds(8 + 2 * x2, 2)]

    def spread_a(o):
        zh2, w2, y2 = (zh + o) % 2, (w + o // 2) % 2, (y + o // 4) % 4
        send(src_a(zh2, w2, y2), held_a.at[mine_a], spread_send.at[0], spread_recv.at[0], place(x, zh2, w2, y2, w))

    def spread_b(o):
        zh2, w2, x2 = (zh + o) % 2, (w + o // 2) % 2, (x + o // 4) % 4
        send(src_b(zh2, w2, x2), held_b.at[mine_b], spread_send.at[1], spread_recv.at[1], place(x2, zh2, w2, y, w))

    def spread_c(o):
        x2, y2, c2 = (x + o // 8) % 4, (y + o // 2) % 4, (c + o) % 2
        send(
            sel.at[c2, :, 16 + x2 * 4 + y2], half_c.at[:, mine_c],
            spread_send.at[2], spread_recv.at[2], place(x2, zh, w, y2, c2),
        )

    def spread(i, carry):
        spread_a((i * 5) % 16)
        spread_b((i * 7) % 16)
        spread_c((i * 2 * 5 + 1) % 32)
        spread_c((i * 2 * 7) % 32)
        return carry

    lax.fori_loop(1, 16, spread, 0)
    spread_c(1)
    pltpu.make_async_copy(sel.at[c, :, 16 + x * 4 + y], half_c.at[:, mine_c], spread_recv.at[2]).start()

    @pl.when(c == w)
    def _():
        pltpu.make_async_copy(src_a(zh, w, y), held_a.at[mine_a], spread_recv.at[0]).start()
        pltpu.make_async_copy(src_b(zh, w, x), held_b.at[mine_b], spread_recv.at[1]).start()

    @pl.when(c != w)
    def _():
        spread_a(0)
        spread_b(0)

    def arrived(ref, sem):
        pltpu.make_async_copy(ref, ref, sem).wait()

    block_a = held_a.at[pl.ds(x * 16, 16)]
    arrived(block_a, spread_recv.at[0])
    for d in (1, 3, 2):
        send(block_a, block_a, ring_send.at[0], ring_recv.at[0], place((x + d) % 4, zh, w, y, c))
    block_b = held_b.at[pl.ds(y * 16, 16)]
    arrived(block_b, spread_recv.at[1])
    for d in (1, 3, 2):
        send(block_b, block_b, ring_send.at[1], ring_recv.at[1], place(x, zh, w, (y + d) % 4, c))
    arrived(half_c, spread_recv.at[2])
    block_c = held_c.at[w, pl.ds(zh * 32, 32)]
    for dzh, dw in ((0, 1), (1, 1), (1, 0)):
        zh2, w2 = (zh + dzh) % 2, (w + dw) % 2
        send(half_c.at[w2], block_c, ring_send.at[2], ring_recv.at[2], place(x, zh2, w2, y, c))
    pltpu.make_async_copy(half_c.at[w], block_c, ring_recv.at[2]).start()

    send(sel.at[:, 1 - w], own.at[:, :, w], own_send, own_recv, place(x, zh, 1 - w, y, c))
    pltpu.make_async_copy(sel.at[:, w], own.at[:, :, w], own_recv).start()

    arrived(held_a.at[pl.ds(0, 48)], ring_recv.at[0])
    arrived(held_b.at[pl.ds(0, 48)], ring_recv.at[1])
    arrived(held_c, ring_recv.at[2])

    bin_c = x * 4 + y

    def fill_a(slot, r, b):
        stage[slot] = held_a[pairing[r, b]]
        return part.at[y, zh, r, :, c]

    def fill_b(slot, r, b):
        p = pairing[r, b]
        stage[slot] = held_b[((p // 2) % 4) * 16 + (p // 8) * 2 + p % 2]
        return part.at[4 + x, zh, r, :, c]

    def fill_c(slot, r, b):
        p = pairing[r, b]
        at = ((p // 8) % 2) * 32 + (p // 16) * 8 + p % 8
        stage[slot, 0] = held_c[0, at]
        stage[slot, 1] = held_c[1, at]
        return part.at[8 + bin_c // 2, c, r, bin_c % 2]

    def give(slot, dst, target):
        send(stage.at[slot], dst, part_send, part_recv, target)

    def give_a(slot, r, o):
        zh2, y2, c2 = (zh + o) % 2, (y + o // 2) % 4, (c + o // 8) % 2
        give(slot, fill_a(slot, r, block_of(x, zh2, y2, c2)), place(x, zh2, w, y2, c2))

    def give_b(slot, r, o):
        zh2, x2, c2 = (zh + o) % 2, (x + o // 2) % 4, (c + o // 8) % 2
        give(slot, fill_b(slot, r, block_of(x2, zh2, y, c2)), place(x2, zh2, w, y, c2))

    def give_c(slot, r, o):
        x2, y2, c2 = (x + o // 8) % 4, (y + o // 2) % 4, (c + o) % 2
        give(slot, fill_c(slot, r, block_of(x2, zh, y2, c2)), place(x2, zh, w, y2, c2))

    def give_round(r, carry):
        def step(i, carry):
            slot = (r * 15 + i - 1) * 4
            give_a(slot, r, (i * 5) % 16)
            give_c(slot + 1, r, (i * 2 * 5 + 1) % 32)
            give_b(slot + 2, r, (i * 7) % 16)
            give_c(slot + 3, r, (i * 2 * 7) % 32)
            return carry

        lax.fori_loop(1, 16, step, 0)
        give_c(rounds * 60 + r, r, 1)
        slot = rounds * 61 + r * 3
        for n, fill in enumerate((fill_a, fill_b, fill_c)):
            pltpu.make_async_copy(stage.at[slot + n], fill(slot + n, r, chan), part_recv).start()
        return carry

    lax.fori_loop(0, rounds, give_round, 0)

    arrived(half_c.at[:, pl.ds(0, 31)], spread_send.at[2])
    for n in range(2):
        @pl.when(c == w)
        def _():
            arrived(held_a.at[pl.ds(0, 15)], spread_send.at[n])

        @pl.when(c != w)
        def _():
            arrived(held_a.at[pl.ds(0, 16)], spread_send.at[n])

        arrived(held_a.at[pl.ds(0, 48)], ring_send.at[n])
    arrived(held_a.at[pl.ds(0, 48)], ring_send.at[2])
    arrived(sel.at[:, 0], own_send)
    arrived(sel, own_recv)
    arrived(stage.at[pl.ds(0, rounds * 61)], part_send)
    arrived(stage, part_recv)


def move(spectra, freq_idx, pairing):
    _, _, width, channels = spectra.shape
    rounds = pairing.shape[0]
    kind = spectra.dtype
    unit = (width, channels)
    return pl.pallas_call(
        move_kernel,
        out_shape=(
            jax.ShapeDtypeStruct((16, 2, rounds, 2, 2) + unit, kind),
            jax.ShapeDtypeStruct((2, 32, 2) + unit, kind),
        ),
        in_specs=[
            pl.BlockSpec(memory_space=pl.ANY),
            pl.BlockSpec(memory_space=pltpu.SMEM),
            pl.BlockSpec(memory_space=pltpu.SMEM),
        ],
        out_specs=(pl.BlockSpec(memory_space=pl.ANY), pl.BlockSpec(memory_space=pl.ANY)),
        scratch_shapes=[
            pltpu.VMEM(spectra.shape, kind),
            pltpu.VMEM((2, 2, 32) + unit, kind),
            pltpu.VMEM((64, 2) + unit, kind),
            pltpu.VMEM((64, 2) + unit, kind),
            pltpu.VMEM((2, 32) + unit, kind),
            pltpu.VMEM((2, 64) + unit, kind),
            pltpu.VMEM((rounds * 64, 2) + unit, kind),
            pltpu.SemaphoreType.DMA,
            pltpu.SemaphoreType.DMA((3,)),
            pltpu.SemaphoreType.DMA((3,)),
            pltpu.SemaphoreType.DMA((3,)),
            pltpu.SemaphoreType.DMA((3,)),
            pltpu.SemaphoreType.DMA,
            pltpu.SemaphoreType.DMA,
            pltpu.SemaphoreType.DMA,
            pltpu.SemaphoreType.DMA,
        ],
        compiler_params=pltpu.CompilerParams(
            collective_id=0, has_side_effects=True, vmem_limit_bytes=32 << 20
        ),
        name="move",
    )(spectra, freq_idx, pairing)


def pair_kernel(scale, own_ref, part_ref, out_ref):
    rounds = part_ref.shape[2]
    channels = own_ref.shape[3]
    for b in range(own_ref.shape[1]):
        real, imag = own_ref[0, b], own_ref[1, b]
        left = jnp.concatenate(
            [jnp.concatenate([real, imag], 0).T, jnp.concatenate([imag, -real], 0).T], 0
        )
        for r in range(0, rounds, 2):
            right = jnp.concatenate(
                [
                    jnp.concatenate([part_ref[0, 0, q, b], part_ref[0, 1, q, b]], 0)
                    for q in (r, r + 1)
                ],
                1,
            )
            product = jnp.dot(left, right, preferred_element_type=jnp.float32) * scale
            product = product.astype(out_ref.dtype)
            for half in range(2):
                for q in range(2):
                    out_ref[half, r + q, b] = product[
                        half * channels : (half + 1) * channels,
                        q * channels : (q + 1) * channels,
                    ]


def pair_products(own, part, scale):
    groups, _, rounds, step, windows, channels = part.shape
    return pl.pallas_call(
        functools.partial(pair_kernel, scale),
        grid=(groups,),
        out_shape=jax.ShapeDtypeStruct((2, rounds, groups * step, channels, channels), own.dtype),
        in_specs=[
            pl.BlockSpec((2, step, windows, channels), lambda i: (0, i, 0, 0)),
            pl.BlockSpec((1, 2, rounds, step, windows, channels), lambda i: (i, 0, 0, 0, 0, 0)),
        ],
        out_specs=pl.BlockSpec((2, rounds, step, channels, channels), lambda i: (0, 0, i, 0, 0)),
        compiler_params=pltpu.CompilerParams(vmem_limit_bytes=32 << 20),
        name="pair_products",
    )(own, part)


def body(spectra, freq_idx, pairing):
    _, _, width, channels = spectra.shape
    rounds = pairing.shape[0]
    scale = 1.0 / math.sqrt(width * lax.axis_size("win"))
    part, own = move(spectra, freq_idx, pairing)
    own = own.reshape(2, 32, 2 * width, channels)
    part = part.reshape(16, 2, rounds, 2, 2 * width, channels)
    return pair_products(own, part, scale)


def solution(mesh):
    return jax.shard_map(
        body,
        mesh=mesh,
        in_specs=(P(None, None, "win", "chan"), P(), P()),
        out_specs=P(None, None, "win", "chan", None),
        check_vma=False,
    )
```

```python
import functools
import math

import jax
import jax.numpy as jnp
from jax import lax
from jax.experimental import pallas as pl
from jax.experimental.pallas import tpu as pltpu
from jax.sharding import PartitionSpec as P

MESH = pl.DeviceIdType.MESH


def block_of(x, zh, y, c):
    return ((x * 2 + zh) * 4 + y) * 2 + c


def place(x, zh, w, y, c):
    return {"chan": block_of(x, zh, y, c), "win": w}


AHEAD = 4
C_STEP = 4


def move_kernel(
    spectra, freq_in, pairing_in, part, left, done,
    whole, freq, pairing, sel, own, held_a, held_b, half_c, held_c, stage,
    load_sem, spread_send, spread_recv, ring_send, ring_recv, far_send, far_recv,
    own_send, own_recv, part_send, part_recv,
):
    chan = lax.axis_index("chan")
    w = lax.axis_index("win")
    c = chan % 2
    y = (chan // 2) % 4
    zh = (chan // 8) % 2
    x = chan // 16
    rounds = pairing.shape[0]

    loads = [
        pltpu.make_async_copy(src, dst, load_sem.at[n])
        for n, (src, dst) in enumerate(((spectra, whole), (freq_in, freq), (pairing_in, pairing)))
    ]
    for load in loads:
        load.start()

    barrier = pltpu.get_barrier_semaphore()

    def greet(dx, dz, dy, dc):
        z = (zh * 2 + w + dz) % 4
        pl.semaphore_signal(
            barrier, inc=1, device_id=place((x + dx) % 4, z // 2, z % 2, (y + dy) % 4, (c + dc) % 2),
            device_id_type=MESH,
        )

    def greet_plane(o, carry):
        dc, one, two = o % 2, (o // 2) % 4, o // 8
        greet(0, one, two, dc)

        @pl.when(two > 0)
        def _():
            greet(two, one, 0, dc)

        @pl.when((one > 0) & (two > 0))
        def _():
            greet(one, 0, two, dc)

        return carry

    lax.fori_loop(1, 32, greet_plane, 0)
    for load in loads:
        load.wait()

    def pick(k, carry):
        f = freq[k]
        for half in range(2):
            sel[half, k // 32, k % 32] = whole[half, f]
        return carry

    lax.fori_loop(0, 64, pick, 0)
    pl.semaphore_wait(barrier, 31 + 24 + 18)

    def send(src, dst, ssem, rsem, target):
        pltpu.make_async_remote_copy(
            src_ref=src, dst_ref=dst, send_sem=ssem, recv_sem=rsem, device_id=target, device_id_type=MESH
        ).start()

    def arrived(ref, sem):
        pltpu.make_async_copy(ref, ref, sem).wait()

    mine_a = block_of(x, zh, y, c)
    mine_b = y * 16 + (x * 2 + zh) * 2 + c
    mine_c = (x * 4 + y) * 2 + c

    def src_a(zh2, w2, y2):
        return sel.at[zh2, w2, pl.ds(2 * y2, 2)]

    def src_b(zh2, w2, x2):
        return sel.at[zh2, w2, pl.ds(8 + 2 * x2, 2)]

    def spread_a(o):
        zh2, w2, y2 = (zh + o) % 2, (w + o // 2) % 2, (y + o // 4) % 4
        send(src_a(zh2, w2, y2), held_a.at[mine_a], spread_send.at[0], spread_recv.at[0], place(x, zh2, w2, y2, w))

    def spread_b(o):
        zh2, w2, x2 = (zh + o) % 2, (w + o // 2) % 2, (x + o // 4) % 4
        send(src_b(zh2, w2, x2), held_b.at[mine_b], spread_send.at[1], spread_recv.at[1], place(x2, zh2, w2, y, w))

    def spread_c(o):
        x2, y2, c2 = (x + o // 8) % 4, (y + o // 2) % 4, (c + o) % 2
        send(
            sel.at[c2, :, 16 + x2 * 4 + y2], half_c.at[:, mine_c],
            spread_send.at[2], spread_recv.at[2], place(x2, zh, w, y2, c2),
        )

    def spread_first(i, carry):
        spread_c((i * 5) % 32)
        return carry

    def spread_rest(i, carry):
        spread_a((i * 5) % 16)
        spread_b((i * 7) % 16)
        return carry

    lax.fori_loop(1, 32, spread_first, 0)
    pltpu.make_async_copy(sel.at[c, :, 16 + x * 4 + y], half_c.at[:, mine_c], spread_recv.at[2]).start()
    lax.fori_loop(1, 16, spread_rest, 0)

    @pl.when(c == w)
    def _():
        pltpu.make_async_copy(src_a(zh, w, y), held_a.at[mine_a], spread_recv.at[0]).start()
        pltpu.make_async_copy(src_b(zh, w, x), held_b.at[mine_b], spread_recv.at[1]).start()

    @pl.when(c != w)
    def _():
        spread_a(0)
        spread_b(0)

    arrived(half_c, spread_recv.at[2])
    block_c = held_c.at[w, pl.ds(zh * 32, 32)]
    for dzh, dw in ((1, 0), (0, 1), (1, 1)):
        zh2, w2 = (zh + dzh) % 2, (w + dw) % 2
        send(half_c.at[w2], block_c, ring_send.at[2], ring_recv.at[4], place(x, zh2, w2, y, c))
    pltpu.make_async_copy(half_c.at[w], block_c, ring_recv.at[4]).start()

    def at_a(d):
        return place((x + d) % 4, zh, w, y, c)

    def at_b(d):
        return place(x, zh, w, (y + d) % 4, c)

    groups = ((held_a, x, at_a), (held_b, y, at_b))
    for n, (held, at, target) in enumerate(groups):
        block = held.at[pl.ds(at * 16, 16)]
        arrived(block, spread_recv.at[n])
        for k, d in enumerate((1, 3)):
            send(block, block, ring_send.at[n], ring_recv.at[2 * n + k], target(d))

    send(sel.at[:, 1 - w], own.at[:, :, w], own_send, own_recv, place(x, zh, 1 - w, y, c))
    pltpu.make_async_copy(sel.at[:, w], own.at[:, :, w], own_recv).start()

    bin_c = x * 4 + y

    def fill_a(slot, r, b):
        stage[slot] = held_a[pairing[r, b]]
        return part.at[r // 2, y, zh, r % 2, :, c]

    def fill_b(slot, r, b):
        p = pairing[r, b]
        stage[slot] = held_b[((p // 2) % 4) * 16 + (p // 8) * 2 + p % 2]
        return part.at[r // 2, 4 + x, zh, r % 2, :, c]

    def fill_c(slot, r, b):
        p = pairing[r, b]
        at = ((p // 8) % 2) * 32 + (p // 16) * 8 + p % 8
        stage[slot, 0] = held_c[0, at]
        stage[slot, 1] = held_c[1, at]
        return part.at[r // 2, 8 + bin_c // 2, c, r % 2, bin_c % 2]

    def give(slot, r, dst, target):
        send(stage.at[slot], dst, part_send, part_recv.at[r // 2], target)

    def give_a(j):
        r, o = j // 15, ((j % 15 + 1) * 5) % 16
        slot = rounds * 31 + j
        zh2, y2, c2 = (zh + o) % 2, (y + o // 2) % 4, (c + o // 8) % 2
        give(slot, r, fill_a(slot, r, block_of(x, zh2, y2, c2)), place(x, zh2, w, y2, c2))

    def give_b(j):
        r, o = j // 15, ((j % 15 + 1) * 7) % 16
        slot = rounds * 46 + j
        zh2, x2, c2 = (zh + o) % 2, (x + o // 2) % 4, (c + o // 8) % 2
        give(slot, r, fill_b(slot, r, block_of(x2, zh2, y, c2)), place(x2, zh2, w, y, c2))

    def give_c(j):
        r, o = j // 31, ((j % 31 + 1) * 5) % 32
        x2, y2, c2 = (x + o // 8) % 4, (y + o // 2) % 4, (c + o) % 2
        give(j, r, fill_c(j, r, block_of(x2, zh, y2, c2)), place(x2, zh, w, y2, c2))

    def keep(r, carry):
        slot = rounds * 61 + r * 3
        for n, fill in enumerate((fill_a, fill_b, fill_c)):
            pltpu.make_async_copy(stage.at[slot + n], fill(slot + n, r, chan), part_recv.at[r // 2]).start()
        return carry

    def give_first(j, carry):
        give_c(j)
        return carry

    first = rounds * 31 - rounds * 5 * C_STEP

    def give_rest(i, carry):
        for n in range(max(3, C_STEP)):
            if n < 3:
                give_a(3 * i + n)
            if n < C_STEP:
                give_c(first + C_STEP * i + n)
            if n < 3:
                give_b(3 * i + n)
        return carry

    for n, (held, at, target) in enumerate(groups):
        for k, d in enumerate((3, 1)):
            arrived(held.at[pl.ds(((at + d) % 4) * 16, 16)], ring_recv.at[2 * n + k])
            half = held.at[pl.ds(((at + d) % 4) * 16 + 8 * k, 8)]
            send(half, half, far_send.at[n], far_recv.at[n], target(4 - d))

    arrived(held_c, ring_recv.at[4])
    lax.fori_loop(0, first, give_first, 0)
    arrived(held_a.at[pl.ds(0, 16)], far_recv.at[0])
    arrived(held_b.at[pl.ds(0, 16)], far_recv.at[1])
    lax.fori_loop(0, rounds * 5, give_rest, 0)
    lax.fori_loop(0, rounds, keep, 0)

    arrived(sel, own_recv)

    def turn(k, carry):
        real = own[0, k].reshape(-1, own.shape[-1])
        imag = own[1, k].reshape(-1, own.shape[-1])
        channels = real.shape[1]
        left[k, :channels] = jnp.concatenate([real, imag], 0).T
        left[k, channels:] = jnp.concatenate([imag, -real], 0).T
        return carry

    lax.fori_loop(0, left.shape[0], turn, 0)
    scale = 1.0 / math.sqrt(own.shape[2] * own.shape[3])
    for pair in range(rounds // 2):
        arrived(part.at[pair], part_recv.at[pair])
        if 2 * pair < AHEAD:
            def multiply(q, carry, pair=pair):
                for b in range(2):
                    products(scale, left, part, done, pair, q, b, 2 * pair)
                return carry

            lax.fori_loop(0, part.shape[1], multiply, 0)

    arrived(half_c.at[:, pl.ds(0, 31)], spread_send.at[2])
    for n in range(2):
        @pl.when(c == w)
        def _():
            arrived(held_a.at[pl.ds(0, 15)], spread_send.at[n])

        @pl.when(c != w)
        def _():
            arrived(held_a.at[pl.ds(0, 16)], spread_send.at[n])

        arrived(held_a.at[pl.ds(0, 32)], ring_send.at[n])
        arrived(held_a.at[pl.ds(0, 16)], far_send.at[n])
    arrived(held_a.at[pl.ds(0, 48)], ring_send.at[2])
    arrived(sel.at[:, 0], own_send)
    arrived(stage.at[pl.ds(0, rounds * 61)], part_send)


def products(scale, left, part, out, pair, q, b, r):
    channels = left.shape[2]
    right = jnp.concatenate(
        [
            jnp.concatenate([part[pair, q, half, n, b].reshape(-1, channels) for half in range(2)], 0)
            for n in range(2)
        ],
        1,
    )
    product = jnp.dot(left[2 * q + b], right, preferred_element_type=jnp.float32) * scale
    product = product.astype(out.dtype)
    for half in range(2):
        for n in range(2):
            out[half, r + n, 2 * q + b] = product[
                half * channels : (half + 1) * channels, n * channels : (n + 1) * channels
            ]


def move(spectra, freq_idx, pairing):
    _, _, width, channels = spectra.shape
    rounds = pairing.shape[0]
    kind = spectra.dtype
    unit = (width, channels)
    return pl.pallas_call(
        move_kernel,
        out_shape=(
            pltpu.VMEM((rounds // 2, 16, 2, 2, 2, 2) + unit, kind),
            pltpu.VMEM((32, 2 * channels, channels), kind),
            pltpu.VMEM((2, AHEAD, 32, channels, channels), kind),
        ),
        in_specs=[pl.BlockSpec(memory_space=pltpu.HBM)] * 3,
        out_specs=(pl.BlockSpec(memory_space=pltpu.VMEM),) * 3,
        scratch_shapes=[
            pltpu.VMEM(spectra.shape, kind),
            pltpu.SMEM(freq_idx.shape, freq_idx.dtype),
            pltpu.SMEM(pairing.shape, pairing.dtype),
            pltpu.VMEM((2, 2, 32) + unit, kind),
            pltpu.VMEM((2, 32, 2) + unit, kind),
            pltpu.VMEM((64, 2) + unit, kind),
            pltpu.VMEM((64, 2) + unit, kind),
            pltpu.VMEM((2, 32) + unit, kind),
            pltpu.VMEM((2, 64) + unit, kind),
            pltpu.VMEM((rounds * 64, 2) + unit, kind),
            pltpu.SemaphoreType.DMA((3,)),
            pltpu.SemaphoreType.DMA((3,)),
            pltpu.SemaphoreType.DMA((3,)),
            pltpu.SemaphoreType.DMA((3,)),
            pltpu.SemaphoreType.DMA((5,)),
            pltpu.SemaphoreType.DMA((2,)),
            pltpu.SemaphoreType.DMA((2,)),
            pltpu.SemaphoreType.DMA,
            pltpu.SemaphoreType.DMA,
            pltpu.SemaphoreType.DMA,
            pltpu.SemaphoreType.DMA((rounds // 2,)),
        ],
        compiler_params=pltpu.CompilerParams(
            collective_id=0, has_side_effects=True, vmem_limit_bytes=40 << 20
        ),
        name="move",
    )(*(pltpu.with_memory_space_constraint(a, pltpu.HBM) for a in (spectra, freq_idx, pairing)))


def finish_kernel(scale, part, left, done, out, rest, sems):
    ahead, last = done.shape[1], rest.shape[1]
    copies = []
    for half in range(2):
        for r in range(ahead):
            copies.append(pltpu.make_async_copy(done.at[half, r], out.at[half, r], sems.at[half, r]))
            copies[-1].start()
    for r in range(0, last, 2):
        def multiply(q, carry, r=r):
            for b in range(2):
                products(scale, left, part, rest, (ahead + r) // 2, q, b, r)
            return carry

        lax.fori_loop(0, part.shape[1], multiply, 0)
        for half in range(2):
            for n in (r, r + 1):
                copies.append(
                    pltpu.make_async_copy(rest.at[half, n], out.at[half, ahead + n], sems.at[half, ahead + n])
                )
                copies[-1].start()
    for copy in copies:
        copy.wait()


def finish(scale, part, left, done):
    rounds = 2 * part.shape[0]
    _, ahead, bins, channels, _ = done.shape
    return pl.pallas_call(
        functools.partial(finish_kernel, scale),
        out_shape=jax.ShapeDtypeStruct((2, rounds, bins, channels, channels), done.dtype),
        in_specs=[pl.BlockSpec(memory_space=pltpu.VMEM)] * 3,
        out_specs=pl.BlockSpec(memory_space=pltpu.HBM),
        scratch_shapes=[
            pltpu.VMEM((2, rounds - ahead, bins, channels, channels), done.dtype),
            pltpu.SemaphoreType.DMA((2, rounds)),
        ],
        compiler_params=pltpu.CompilerParams(vmem_limit_bytes=16 << 20),
        name="finish",
    )(part, left, done)


def body(spectra, freq_idx, pairing):
    scale = 1.0 / math.sqrt(spectra.shape[2] * lax.axis_size("win"))
    part, left, done = move(spectra, freq_idx, pairing)
    return finish(scale, part, left, done)


def solution(mesh):
    return jax.shard_map(
        body,
        mesh=mesh,
        in_specs=(P(None, None, "win", "chan"), P(), P()),
        out_specs=P(None, None, "win", "chan", None),
        check_vma=False,
    )
```

```python
import functools
import math

import jax
import jax.numpy as jnp
from jax import lax
from jax.experimental import pallas as pl
from jax.experimental.pallas import tpu as pltpu
from jax.sharding import PartitionSpec as P

MESH = pl.DeviceIdType.MESH


def block_of(x, zh, y, c):
    return ((x * 2 + zh) * 4 + y) * 2 + c


def place(x, zh, w, y, c):
    return {"chan": block_of(x, zh, y, c), "win": w}


AHEAD = 4
PIECES = 4
SIDE_BINS = 4
DEEP_BINS = 4
SIDE = ((0, 1), (1, 3))
DEEP = ((0, 1), (1, 3))


def move_kernel(
    spectra, freq_in, pairing_in, part, left, done,
    whole, freq, pairing, sel, own,
    held_a0, held_a1, held_b0, held_b1, half_c0, half_c1, held_c0, held_c1,
    stage_a0, stage_a1, stage_b0, stage_b1, stage_c0, stage_c1,
    load_sem, spread_send, spread_recv, ring_send, ring_recv, near_send, near_recv,
    far_send, far_recv, own_send, own_recv, part_send, part_recv,
):
    held_a, held_b, half_c, held_c = (held_a0, held_a1), (held_b0, held_b1), (half_c0, half_c1), (held_c0, held_c1)
    stage_a, stage_b, stage_c = (stage_a0, stage_a1), (stage_b0, stage_b1), (stage_c0, stage_c1)
    chan = lax.axis_index("chan")
    w = lax.axis_index("win")
    c = chan % 2
    y = (chan // 2) % 4
    zh = (chan // 8) % 2
    x = chan // 16
    pairs = pairing.shape[0] // 2
    first_b, first_c = 2 * SIDE_BINS, 4 * SIDE_BINS

    loads = [
        pltpu.make_async_copy(src, dst, load_sem.at[n])
        for n, (src, dst) in enumerate(((spectra, whole), (freq_in, freq), (pairing_in, pairing)))
    ]
    for load in loads:
        load.start()

    barrier = pltpu.get_barrier_semaphore()

    def greet(dx, dz, dy, dc):
        z = (zh * 2 + w + dz) % 4
        pl.semaphore_signal(
            barrier, inc=1, device_id=place((x + dx) % 4, z // 2, z % 2, (y + dy) % 4, (c + dc) % 2),
            device_id_type=MESH,
        )

    def greet_plane(o, carry):
        dc, one, two = o % 2, (o // 2) % 4, o // 8
        greet(0, one, two, dc)

        @pl.when(two > 0)
        def _():
            greet(two, one, 0, dc)

        @pl.when((one > 0) & (two > 0))
        def _():
            greet(one, 0, two, dc)

        return carry

    lax.fori_loop(1, 32, greet_plane, 0)
    for load in loads:
        load.wait()

    def pick(k, carry):
        f = freq[k]
        for half in range(2):
            sel[half, k // 32, k % 32] = whole[half, f]
        return carry

    lax.fori_loop(0, 64, pick, 0)
    pl.semaphore_wait(barrier, 31 + 24 + 18)

    def send(src, dst, ssem, rsem, target):
        pltpu.make_async_remote_copy(
            src_ref=src, dst_ref=dst, send_sem=ssem, recv_sem=rsem, device_id=target, device_id_type=MESH
        ).start()

    def arrived(ref, sem):
        pltpu.make_async_copy(ref, ref, sem).wait()

    mine_a = block_of(x, zh, y, c)
    mine_b = y * 16 + (x * 2 + zh) * 2 + c
    mine_c = (x * 4 + y) * 2 + c

    def src_a(t, zh2, w2, y2):
        start, size = SIDE[t]
        return sel.at[y2 // 2, w2, pl.ds(SIDE_BINS * (y2 % 2) + start, size), zh2]

    def src_b(t, zh2, w2, x2):
        start, size = SIDE[t]
        return sel.at[x2 // 2, w2, pl.ds(first_b + SIDE_BINS * (x2 % 2) + start, size), zh2]

    def src_c(t, x2, y2):
        start, size = DEEP[t]
        return sel.at[x2 // 2, :, pl.ds(first_c + DEEP_BINS * y2 + start, size), x2 % 2]

    def spread_a(t, o):
        zh2, w2, y2 = (zh + o) % 2, (w + o // 2) % 2, (y + o // 4) % 4
        send(
            src_a(t, zh2, w2, y2), held_a[t].at[mine_a],
            spread_send.at[t, 0], spread_recv.at[t, 0], place(x, zh2, w2, y2, w),
        )

    def spread_b(t, o):
        zh2, w2, x2 = (zh + o) % 2, (w + o // 2) % 2, (x + o // 4) % 4
        send(
            src_b(t, zh2, w2, x2), held_b[t].at[mine_b],
            spread_send.at[t, 1], spread_recv.at[t, 1], place(x2, zh2, w2, y, w),
        )

    def spread_c(t, o):
        x2, y2 = (x + o // 4) % 4, (y + o) % 4
        send(
            src_c(t, x2, y2), half_c[t].at[:, mine_c],
            spread_send.at[t, 2], spread_recv.at[t, 2], place(x2, zh, w, y2, w),
        )

    for t in range(2):
        def spread(i, carry, t=t):
            spread_c(t, (i * 5) % 16)
            spread_a(t, (i * 5) % 16)
            spread_b(t, (i * 7) % 16)
            return carry

        lax.fori_loop(1, 16, spread, 0)

        @pl.when(c == w)
        def _():
            pltpu.make_async_copy(src_a(t, zh, w, y), held_a[t].at[mine_a], spread_recv.at[t, 0]).start()
            pltpu.make_async_copy(src_b(t, zh, w, x), held_b[t].at[mine_b], spread_recv.at[t, 1]).start()
            pltpu.make_async_copy(src_c(t, x, y), half_c[t].at[:, mine_c], spread_recv.at[t, 2]).start()

        @pl.when(c != w)
        def _():
            spread_c(t, 0)
            spread_a(t, 0)
            spread_b(t, 0)

    def at_a(d):
        return place((x + d) % 4, zh, w, y, c)

    def at_b(d):
        return place(x, zh, w, (y + d) % 4, c)

    groups = ((held_a, x, at_a), (held_b, y, at_b))

    def pass_on(t):
        @pl.when(c == w)
        def _():
            arrived(half_c[t], spread_recv.at[t, 2])
            block = held_c[t].at[pl.ds(zh * 32, 32)]
            for n, (dzh, dw) in enumerate(((1, 0), (0, 1), (1, 1))):
                zh2, w2 = (zh + dzh) % 2, (w + dw) % 2
                send(half_c[t].at[w2], block, near_send.at[t, n], near_recv.at[t], place(x, zh2, w2, y, c))
            pltpu.make_async_copy(half_c[t].at[w], block, near_recv.at[t]).start()

        for n, (held, at, target) in enumerate(groups):
            block = held[t].at[pl.ds(at * 16, 16)]
            arrived(block, spread_recv.at[t, n])
            for k, d in enumerate((1, 3)):
                send(block, block, ring_send.at[t, n], ring_recv.at[t, n, k], target(d))

    def pass_far(t):
        for n, (held, at, target) in enumerate(groups):
            for k, d in enumerate((3, 1)):
                arrived(held[t].at[pl.ds(((at + d) % 4) * 16, 16)], ring_recv.at[t, n, k])
                half = held[t].at[pl.ds(((at + d) % 4) * 16 + 8 * k, 8)]
                send(half, half, far_send.at[t, n], far_recv.at[t, n], target(4 - d))

    def pass_end(t):
        for n, (held, at, target) in enumerate(groups):
            arrived(held[t].at[pl.ds(0, 16)], far_recv.at[t, n])
        arrived(held_c[t], near_recv.at[t])

    def fill_a(t, slot, pair, b):
        start, size = SIDE[t]
        for n in range(2):
            stage_a[t][slot, :, n] = held_a[t][pairing[2 * pair + n, b]]
        return part.at[pair, pl.ds(SIDE_BINS * (y % 2) + start, size), y // 2, :, c, zh]

    def fill_b(t, slot, pair, b):
        start, size = SIDE[t]
        for n in range(2):
            p = pairing[2 * pair + n, b]
            stage_b[t][slot, :, n] = held_b[t][((p // 2) % 4) * 16 + (p // 8) * 2 + p % 2]
        return part.at[pair, pl.ds(first_b + SIDE_BINS * (x % 2) + start, size), x // 2, :, c, zh]

    def fill_c(t, slot, pair, b):
        start, size = DEEP[t]
        for n in range(2):
            p = pairing[2 * pair + n, b]
            stage_c[t][slot, :, n] = held_c[t][((p // 8) % 2) * 32 + (p // 16) * 8 + p % 8]
        return part.at[pair, pl.ds(first_c + DEEP_BINS * y + start, size), x // 2, :, c, x % 2]

    def give_a(t, j):
        pair, o = j // 15, ((j % 15 + 1) * 5) % 16
        zh2, y2, c2 = (zh + o) % 2, (y + o // 2) % 4, (c + o // 8) % 2
        dst = fill_a(t, j, pair, block_of(x, zh2, y2, c2))
        send(stage_a[t].at[j], dst, part_send.at[t, 0], part_recv.at[pair], place(x, zh2, w, y2, c2))

    def give_b(t, j):
        pair, o = j // 15, ((j % 15 + 1) * 7) % 16
        zh2, x2, c2 = (zh + o) % 2, (x + o // 2) % 4, (c + o // 8) % 2
        dst = fill_b(t, j, pair, block_of(x2, zh2, y, c2))
        send(stage_b[t].at[j], dst, part_send.at[t, 1], part_recv.at[pair], place(x2, zh2, w, y, c2))

    def give_c(t, j):
        pair, o = j // 31, ((j % 31 + 1) * 5) % 32
        x2, y2, c2 = (x + o // 8) % 4, (y + o // 2) % 4, (c + o) % 2
        dst = fill_c(t, j, pair, block_of(x2, zh, y2, c2))
        send(stage_c[t].at[j], dst, part_send.at[t, 2], part_recv.at[pair], place(x2, zh, w, y2, c2))

    def give(t, begin, end):
        def step(i, carry):
            for n in range(3):
                give_c(t, pairs + 6 * i + 2 * n)
                give_a(t, 3 * i + n)
                give_c(t, pairs + 6 * i + 2 * n + 1)
                give_b(t, 3 * i + n)
            return carry

        lax.fori_loop(begin, end, step, 0)

    def keep(t):
        def step(pair, carry):
            for stage, fill, others in (
                (stage_a, fill_a, 15), (stage_b, fill_b, 15), (stage_c, fill_c, 31)
            ):
                slot = others * pairs + pair
                dst = fill(t, slot, pair, chan)
                pltpu.make_async_copy(stage[t].at[slot], dst, part_recv.at[pair]).start()
            give_c(t, pair)
            return carry

        lax.fori_loop(0, pairs, step, 0)

    turns = 5 * pairs
    pass_on(0)
    pass_far(0)
    pass_on(1)
    pass_end(0)
    keep(0)
    give(0, 0, turns // 2)
    pass_far(1)
    send(sel.at[:, 1 - w], own.at[:, :, w], own_send, own_recv, place(x, zh, 1 - w, y, c))
    pltpu.make_async_copy(sel.at[:, w], own.at[:, :, w], own_recv).start()
    give(0, turns // 2, turns)
    pass_end(1)
    keep(1)
    give(1, 0, turns)

    arrived(sel, own_recv)

    def turn(k, carry):
        real = own[0, k].reshape(-1, own.shape[-1])
        imag = own[1, k].reshape(-1, own.shape[-1])
        channels = real.shape[1]
        left[k, :channels] = jnp.concatenate([real, imag], 0).T
        left[k, channels:] = jnp.concatenate([imag, -real], 0).T
        return carry

    lax.fori_loop(0, left.shape[0], turn, 0)
    scale = 1.0 / math.sqrt(own.shape[2] * own.shape[3] * own.shape[4])
    for pair in range(pairs):
        arrived(part.at[pair], part_recv.at[pair])
        if 2 * pair < AHEAD:
            def multiply(q, carry, pair=pair):
                for b in range(2):
                    products(scale, left, part, done, pair, q, b, 2 * pair)
                return carry

            lax.fori_loop(0, part.shape[1] // 2, multiply, 0)

    for t in range(2):
        def gone(others, t=t):
            arrived(held_a[t].at[pl.ds(0, others)], spread_send.at[t, 0])
            arrived(held_b[t].at[pl.ds(0, others)], spread_send.at[t, 1])
            arrived(half_c[t].at[:, pl.ds(0, others)], spread_send.at[t, 2])

        @pl.when(c == w)
        def _():
            gone(15)
            for n in range(3):
                arrived(held_c[t].at[pl.ds(0, 32)], near_send.at[t, n])

        @pl.when(c != w)
        def _():
            gone(16)

        for n in range(2):
            arrived(held_a[t].at[pl.ds(0, 32)], ring_send.at[t, n])
            arrived(held_a[t].at[pl.ds(0, 16)], far_send.at[t, n])
        for n, (stage, others) in enumerate(((stage_a, 15), (stage_b, 15), (stage_c, 31))):
            arrived(stage[t].at[pl.ds(0, others * pairs)], part_send.at[t, n])
    arrived(sel.at[:, 0], own_send)


def products(scale, left, part, out, pair, q, b, r):
    channels = left.shape[2]
    right = jnp.concatenate(
        [
            jnp.concatenate([part[pair, 2 * q + b, half, n].reshape(-1, channels) for half in range(2)], 0)
            for n in range(2)
        ],
        1,
    )
    product = jnp.dot(left[2 * q + b], right, preferred_element_type=jnp.float32) * scale
    product = product.astype(out.dtype)
    for half in range(2):
        for n in range(2):
            out[half, r + n, 2 * q + b] = product[
                half * channels : (half + 1) * channels, n * channels : (n + 1) * channels
            ]


def move(spectra, freq_idx, pairing):
    _, nbins, width, channels = spectra.shape
    rounds = pairing.shape[0]
    kind = spectra.dtype
    tile = (width // 2, channels)
    spectra = spectra.reshape((2, nbins, 2) + tile)
    side, deep = [n for _, n in SIDE], [n for _, n in DEEP]
    return pl.pallas_call(
        move_kernel,
        out_shape=(
            pltpu.VMEM((rounds // 2, 32, 2, 2, 2, 2) + tile, kind),
            pltpu.VMEM((32, 2 * channels, channels), kind),
            pltpu.VMEM((2, AHEAD, 32, channels, channels), kind),
        ),
        in_specs=[pl.BlockSpec(memory_space=pltpu.HBM)] * 3,
        out_specs=(pl.BlockSpec(memory_space=pltpu.VMEM),) * 3,
        scratch_shapes=[
            pltpu.VMEM(spectra.shape, kind),
            pltpu.SMEM(freq_idx.shape, freq_idx.dtype),
            pltpu.SMEM(pairing.shape, pairing.dtype),
            pltpu.VMEM((2, 2, 32, 2) + tile, kind),
            pltpu.VMEM((2, 32, 2, 2) + tile, kind),
            *[pltpu.VMEM((64, n) + tile, kind) for n in side],
            *[pltpu.VMEM((64, n) + tile, kind) for n in side],
            *[pltpu.VMEM((2, 32, n) + tile, kind) for n in deep],
            *[pltpu.VMEM((64, n) + tile, kind) for n in deep],
            *[pltpu.VMEM((8 * rounds, n, 2) + tile, kind) for n in side],
            *[pltpu.VMEM((8 * rounds, n, 2) + tile, kind) for n in side],
            *[pltpu.VMEM((16 * rounds, n, 2) + tile, kind) for n in deep],
            pltpu.SemaphoreType.DMA((3,)),
            pltpu.SemaphoreType.DMA((2, 3)),
            pltpu.SemaphoreType.DMA((2, 3)),
            pltpu.SemaphoreType.DMA((2, 2)),
            pltpu.SemaphoreType.DMA((2, 2, 2)),
            pltpu.SemaphoreType.DMA((2, 3)),
            pltpu.SemaphoreType.DMA((2,)),
            pltpu.SemaphoreType.DMA((2, 2)),
            pltpu.SemaphoreType.DMA((2, 2)),
            pltpu.SemaphoreType.DMA,
            pltpu.SemaphoreType.DMA,
            pltpu.SemaphoreType.DMA((2, 3)),
            pltpu.SemaphoreType.DMA((rounds // 2,)),
        ],
        compiler_params=pltpu.CompilerParams(
            collective_id=0, has_side_effects=True, vmem_limit_bytes=40 << 20
        ),
        name="move",
    )(*(pltpu.with_memory_space_constraint(a, pltpu.HBM) for a in (spectra, freq_idx, pairing)))


def finish_kernel(scale, part, left, done, out, rest, sems, rest_sems):
    ahead, last = done.shape[1], rest.shape[1]
    copies = []
    for half in range(2):
        for r in range(ahead):
            copies.append(pltpu.make_async_copy(done.at[half, r], out.at[half, r], sems.at[half, r]))
            copies[-1].start()
    groups = part.shape[1] // 2
    for r in range(0, last, 2):
        for piece in range(PIECES):
            def multiply(q, carry, r=r):
                for b in range(2):
                    products(scale, left, part, rest, (ahead + r) // 2, q, b, r)
                return carry

            size = groups // PIECES
            lax.fori_loop(piece * size, (piece + 1) * size, multiply, 0)
            bins = pl.ds(piece * size * 2, size * 2)
            for half in range(2):
                copies.append(
                    pltpu.make_async_copy(
                        rest.at[half, pl.ds(r, 2), bins],
                        out.at[half, pl.ds(ahead + r, 2), bins],
                        rest_sems.at[r // 2, half, piece],
                    )
                )
                copies[-1].start()
    for copy in copies:
        copy.wait()


def finish(scale, part, left, done):
    rounds = 2 * part.shape[0]
    _, ahead, bins, channels, _ = done.shape
    return pl.pallas_call(
        functools.partial(finish_kernel, scale),
        out_shape=jax.ShapeDtypeStruct((2, rounds, bins, channels, channels), done.dtype),
        in_specs=[pl.BlockSpec(memory_space=pltpu.VMEM)] * 3,
        out_specs=pl.BlockSpec(memory_space=pltpu.HBM),
        scratch_shapes=[
            pltpu.VMEM((2, rounds - ahead, bins, channels, channels), done.dtype),
            pltpu.SemaphoreType.DMA((2, ahead)),
            pltpu.SemaphoreType.DMA(((rounds - ahead) // 2, 2, PIECES)),
        ],
        compiler_params=pltpu.CompilerParams(vmem_limit_bytes=16 << 20),
        name="finish",
    )(part, left, done)


def body(spectra, freq_idx, pairing):
    scale = 1.0 / math.sqrt(spectra.shape[2] * lax.axis_size("win"))
    part, left, done = move(spectra, freq_idx, pairing)
    return finish(scale, part, left, done)


def solution(mesh):
    return jax.shard_map(
        body,
        mesh=mesh,
        in_specs=(P(None, None, "win", "chan"), P(), P()),
        out_specs=P(None, None, "win", "chan", None),
        check_vma=False,
    )
```

```python
import functools
import math

import jax
import jax.numpy as jnp
from jax import lax
from jax.experimental import pallas as pl
from jax.experimental.pallas import tpu as pltpu
from jax.sharding import PartitionSpec as P

MESH = pl.DeviceIdType.MESH


def block_of(x, zh, y, c):
    return ((x * 2 + zh) * 4 + y) * 2 + c


def place(x, zh, w, y, c):
    return {"chan": block_of(x, zh, y, c), "win": w}


AHEAD = 4
PIECES = 4
BINS = 4
CUTS = ((0, 1), (1, 3))


def move_kernel(
    spectra, freq_in, pairing_in, part, left, done,
    whole, freq, pairing, sel, own,
    held_a0, held_a1, held_b0, held_b1, held_c0, held_c1, held_d0, held_d1,
    half_c0, half_c1, half_d0, half_d1,
    stage_a0, stage_a1, stage_b0, stage_b1, stage_c0, stage_c1, stage_d0, stage_d1,
    load_sem, spread_send, spread_recv, ring_send, ring_recv, far_send, far_recv, near_send, near_recv,
    mate_send, mate_recv, own_send, own_recv, part_send, part_recv,
):
    held = ((held_a0, held_a1), (held_b0, held_b1), (held_c0, held_c1), (held_d0, held_d1))
    half = ((half_c0, half_c1), (half_d0, half_d1))
    stage = ((stage_a0, stage_a1), (stage_b0, stage_b1), (stage_c0, stage_c1), (stage_d0, stage_d1))
    chan = lax.axis_index("chan")
    w = lax.axis_index("win")
    c = chan % 2
    y = (chan // 2) % 4
    zh = (chan // 8) % 2
    x = chan // 16
    pairs = pairing.shape[0] // 2

    loads = [
        pltpu.make_async_copy(src, dst, load_sem.at[n])
        for n, (src, dst) in enumerate(((spectra, whole), (freq_in, freq), (pairing_in, pairing)))
    ]
    for load in loads:
        load.start()

    barrier = pltpu.get_barrier_semaphore()

    def greet(dx, dz, dy, dc):
        z = (zh * 2 + w + dz) % 4
        pl.semaphore_signal(
            barrier, inc=1, device_id=place((x + dx) % 4, z // 2, z % 2, (y + dy) % 4, (c + dc) % 2),
            device_id_type=MESH,
        )

    def greet_plane(o, carry):
        dc, one, two = o % 2, (o // 2) % 4, o // 8
        greet(0, one, two, dc)

        @pl.when(two > 0)
        def _():
            greet(two, one, 0, dc)

        @pl.when((one > 0) & (two > 0))
        def _():
            greet(one, 0, two, dc)

        return carry

    lax.fori_loop(1, 32, greet_plane, 0)
    for load in loads:
        load.wait()

    def pick(k, carry):
        f = freq[k]
        for half in range(2):
            sel[half, k // 32, k % 32] = whole[half, f]
        return carry

    lax.fori_loop(0, 64, pick, 0, unroll=8)
    pl.semaphore_wait(barrier, 31 + 24 + 18)

    def send(src, dst, ssem, rsem, target):
        pltpu.make_async_remote_copy(
            src_ref=src, dst_ref=dst, send_sem=ssem, recv_sem=rsem, device_id=target, device_id_type=MESH
        ).start()

    def arrived(ref, sem):
        pltpu.make_async_copy(ref, ref, sem).wait()

    def bins_of(n, t, group):
        start, size = CUTS[t]
        return pl.ds((2 * n + group) * BINS + start, size)

    def chunk_of(n, zh2, x2, y2, core):
        major = y2 if n in (0, 2) else x2
        minor = (zh2, zh2, pair_of(x2, core), pair_of(y2, core))[n]
        return major % 2, major // 2, minor

    def pick_by(core, zero, one):
        return (1 - core) * zero + core * one

    def across(at, bit, core):
        return at + bit * pick_by(core, 3 - 2 * at, 1 - 2 * (at % 2))

    def pair_of(at, core):
        return pick_by(core, at // 2, ((at + 1) // 2) % 2)

    def side_of(at, core):
        return pair_of(at, 1 - core)

    def index_of(n, p):
        x2, zh2, y2, c2 = p // 16, (p // 8) % 2, (p // 2) % 4, p % 2
        if n == 0:
            return p
        if n == 1:
            return y2 * 16 + x2 * 4 + zh2 * 2 + c2
        if n == 2:
            return side_of(x2, c) * 32 + zh2 * 16 + pair_of(x2, c) * 8 + y2 * 2 + c2
        return side_of(y2, c) * 32 + zh2 * 16 + pair_of(y2, c) * 8 + x2 * 2 + c2

    mine_half = (pair_of(x, w) * 8 + y * 2 + c, pair_of(y, w) * 8 + x * 2 + c)

    def source(n, t, zh2, w2, x2, y2):
        group, part_half, windows = chunk_of(n, zh2, x2, y2, w)
        return sel.at[part_half, w2 if n < 2 else slice(None), bins_of(n, t, group), windows]

    def landing(n, t):
        return held[n][t].at[index_of(n, chan)] if n < 2 else half[n - 2][t].at[:, mine_half[n - 2]]

    def spread_to(n, o):
        if n == 0:
            return (zh + o) % 2, (w + o // 2) % 2, x, (y + o // 4) % 4
        if n == 1:
            return (zh + o) % 2, (w + o // 2) % 2, (x + o // 4) % 4, y
        if n == 2:
            return zh, w, across(x, o % 2, w), (y + o // 2) % 4
        return zh, w, (x + o // 2) % 4, across(y, o % 2, w)

    def spread_one(n, t, o):
        zh2, w2, x2, y2 = spread_to(n, o)
        send(
            source(n, t, zh2, w2, x2, y2), landing(n, t),
            spread_send.at[t, n], spread_recv.at[t, n], place(x2, zh2, w2, y2, w),
        )

    for t in range(2):
        def spread(i, carry, t=t):
            spread_one(2, t, (i * 3) % 8)
            spread_one(0, t, (i * 10) % 16)
            spread_one(1, t, (i * 14) % 16)
            spread_one(3, t, (i * 5) % 8)
            spread_one(0, t, (i * 10 + 5) % 16)
            spread_one(1, t, (i * 14 + 7) % 16)
            return carry

        lax.fori_loop(1, 8, spread, 0)
        spread_one(0, t, 5)
        spread_one(1, t, 7)

        @pl.when(c == w)
        def _():
            for n in range(4):
                pltpu.make_async_copy(source(n, t, zh, w, x, y), landing(n, t), spread_recv.at[t, n]).start()

        @pl.when(c != w)
        def _():
            for n in range(4):
                spread_one(n, t, 0)

    def line(n, d):
        return place((x + d) % 4, zh, w, y, c) if n == 0 else place(x, zh, w, (y + d) % 4, c)

    sides = (side_of(x, c), side_of(y, c))
    mates = (place(across(x, 1, 1 - c), zh, w, y, c), place(x, zh, w, across(y, 1, 1 - c), c))

    def pass_on(t):
        @pl.when(c == w)
        def _():
            for n in range(2):
                arrived(half[n][t], spread_recv.at[t, 2 + n])
                block = held[2 + n][t].at[pl.ds(sides[n] * 32 + zh * 16, 16)]
                for k, (dzh, dw) in enumerate(((1, 0), (0, 1), (1, 1))):
                    zh2, w2 = (zh + dzh) % 2, (w + dw) % 2
                    send(half[n][t].at[w2], block, near_send.at[t, n, k], near_recv.at[t, n], place(x, zh2, w2, y, c))
                pltpu.make_async_copy(half[n][t].at[w], block, near_recv.at[t, n]).start()

        for n, at in enumerate((x, y)):
            block = held[n][t].at[pl.ds(at * 16, 16)]
            arrived(block, spread_recv.at[t, n])
            for k, d in enumerate((1, 3)):
                send(block, block, ring_send.at[t, n], ring_recv.at[t, n, k], line(n, d))

    def pass_far(t):
        for n, at in enumerate((x, y)):
            for k, d in enumerate((3, 1)):
                arrived(held[n][t].at[pl.ds(((at + d) % 4) * 16, 16)], ring_recv.at[t, n, k])
                block = held[n][t].at[pl.ds(((at + d) % 4) * 16 + 8 * k, 8)]
                send(block, block, far_send.at[t, n], far_recv.at[t, n], line(n, 4 - d))
        for n in range(2):
            block = held[2 + n][t].at[pl.ds(sides[n] * 32, 32)]
            arrived(block, near_recv.at[t, n])
            send(block, block, mate_send.at[t, n], mate_recv.at[t, n], mates[n])

    def pass_end(t):
        for n in range(2):
            arrived(held[n][t].at[pl.ds(0, 16)], far_recv.at[t, n])
            arrived(held[2 + n][t].at[pl.ds(0, 32)], mate_recv.at[t, n])

    def fill(n, t, slot, pair, b):
        for k in range(2):
            stage[n][t][slot, :, k] = held[n][t][index_of(n, pairing[2 * pair + k, b])]
        group, part_half, windows = chunk_of(n, zh, x, y, c)
        return part.at[pair, bins_of(n, t, group), part_half, :, c, windows]

    def give_one(n, t, j):
        pair, o = j // 15, ((j % 15 + 1) * (5, 7, 11, 13)[n]) % 16
        c2 = (c + o // 8) % 2
        zh2, x2, y2 = (
            ((zh + o) % 2, x, (y + o // 2) % 4),
            ((zh + o // 4) % 2, (x + o) % 4, y),
            (zh, across(x, (o // 4) % 2, c), (y + o) % 4),
            (zh, (x + o // 2) % 4, across(y, o % 2, c)),
        )[n]
        dst = fill(n, t, j, pair, block_of(x2, zh2, y2, c2))
        send(stage[n][t].at[j], dst, part_send.at[t, n], part_recv.at[pair], place(x2, zh2, w, y2, c2))

    def give(t, begin, end):
        def step(i, carry):
            for k in range(3):
                for n in (0, 2, 1, 3):
                    give_one(n, t, 3 * i + k)
            return carry

        lax.fori_loop(begin, end, step, 0)

    def keep(t):
        def step(pair, carry):
            for n in range(4):
                slot = 15 * pairs + pair
                dst = fill(n, t, slot, pair, chan)
                pltpu.make_async_copy(stage[n][t].at[slot], dst, part_recv.at[pair]).start()
            return carry

        lax.fori_loop(0, pairs, step, 0)

    turns = 5 * pairs
    pass_on(0)
    pass_far(0)
    pass_on(1)
    pass_end(0)
    keep(0)
    give(0, 0, turns // 5)
    pass_far(1)
    send(sel.at[:, 1 - w], own.at[:, :, w], own_send, own_recv, place(x, zh, 1 - w, y, c))
    pltpu.make_async_copy(sel.at[:, w], own.at[:, :, w], own_recv).start()
    give(0, turns // 5, turns)
    pass_end(1)
    keep(1)
    give(1, 0, turns)

    arrived(sel, own_recv)

    def turn(k, carry):
        real = own[0, k].reshape(-1, own.shape[-1])
        imag = own[1, k].reshape(-1, own.shape[-1])
        channels = real.shape[1]
        left[k, :channels] = jnp.concatenate([real, imag], 0).T
        left[k, channels:] = jnp.concatenate([imag, -real], 0).T
        return carry

    lax.fori_loop(0, left.shape[0], turn, 0)
    scale = 1.0 / math.sqrt(own.shape[2] * own.shape[3] * own.shape[4])
    for pair in range(pairs):
        arrived(part.at[pair], part_recv.at[pair])
        if 2 * pair < AHEAD:
            def multiply(q, carry, pair=pair):
                for b in range(2):
                    products(scale, left, part, done, pair, q, b, 2 * pair)
                return carry

            lax.fori_loop(0, part.shape[1] // 2, multiply, 0)

    for t in range(2):
        def gone(missing, t=t):
            for n in range(2):
                arrived(held[n][t].at[pl.ds(0, 16 - missing)], spread_send.at[t, n])
                arrived(half[n][t].at[:, pl.ds(0, 8 - missing)], spread_send.at[t, 2 + n])

        @pl.when(c == w)
        def _():
            gone(1)
            for n in range(2):
                for k in range(3):
                    arrived(held[2 + n][t].at[pl.ds(0, 16)], near_send.at[t, n, k])

        @pl.when(c != w)
        def _():
            gone(0)

        for n in range(2):
            arrived(held[n][t].at[pl.ds(0, 32)], ring_send.at[t, n])
            arrived(held[n][t].at[pl.ds(0, 16)], far_send.at[t, n])
            arrived(held[2 + n][t].at[pl.ds(0, 32)], mate_send.at[t, n])
        for n in range(4):
            arrived(stage[n][t].at[pl.ds(0, 15 * pairs)], part_send.at[t, n])
    arrived(sel.at[:, 0], own_send)


def products(scale, left, part, out, pair, q, b, r):
    channels = left.shape[2]
    right = jnp.concatenate(
        [
            jnp.concatenate([part[pair, 2 * q + b, half, n].reshape(-1, channels) for half in range(2)], 0)
            for n in range(2)
        ],
        1,
    )
    product = jnp.dot(left[2 * q + b], right, preferred_element_type=jnp.float32) * scale
    product = product.astype(out.dtype)
    for half in range(2):
        for n in range(2):
            out[half, r + n, 2 * q + b] = product[
                half * channels : (half + 1) * channels, n * channels : (n + 1) * channels
            ]


def move(spectra, freq_idx, pairing):
    _, nbins, width, channels = spectra.shape
    rounds = pairing.shape[0]
    kind = spectra.dtype
    tile = (width // 2, channels)
    spectra = spectra.reshape((2, nbins, 2) + tile)
    sizes = [n for _, n in CUTS]
    return pl.pallas_call(
        move_kernel,
        out_shape=(
            pltpu.VMEM((rounds // 2, 32, 2, 2, 2, 2) + tile, kind),
            pltpu.VMEM((32, 2 * channels, channels), kind),
            pltpu.VMEM((2, AHEAD, 32, channels, channels), kind),
        ),
        in_specs=[pl.BlockSpec(memory_space=pltpu.HBM)] * 3,
        out_specs=(pl.BlockSpec(memory_space=pltpu.VMEM),) * 3,
        scratch_shapes=[
            pltpu.VMEM(spectra.shape, kind),
            pltpu.SMEM(freq_idx.shape, freq_idx.dtype),
            pltpu.SMEM(pairing.shape, pairing.dtype),
            pltpu.VMEM((2, 2, 32, 2) + tile, kind),
            pltpu.VMEM((2, 32, 2, 2) + tile, kind),
            *[pltpu.VMEM((64, n) + tile, kind) for _ in range(4) for n in sizes],
            *[pltpu.VMEM((2, 16, n) + tile, kind) for _ in range(2) for n in sizes],
            *[pltpu.VMEM((8 * rounds, n, 2) + tile, kind) for _ in range(4) for n in sizes],
            pltpu.SemaphoreType.DMA((3,)),
            pltpu.SemaphoreType.DMA((2, 4)),
            pltpu.SemaphoreType.DMA((2, 4)),
            pltpu.SemaphoreType.DMA((2, 2)),
            pltpu.SemaphoreType.DMA((2, 2, 2)),
            pltpu.SemaphoreType.DMA((2, 2)),
            pltpu.SemaphoreType.DMA((2, 2)),
            pltpu.SemaphoreType.DMA((2, 2, 3)),
            pltpu.SemaphoreType.DMA((2, 2)),
            pltpu.SemaphoreType.DMA((2, 2)),
            pltpu.SemaphoreType.DMA((2, 2)),
            pltpu.SemaphoreType.DMA,
            pltpu.SemaphoreType.DMA,
            pltpu.SemaphoreType.DMA((2, 4)),
            pltpu.SemaphoreType.DMA((rounds // 2,)),
        ],
        compiler_params=pltpu.CompilerParams(
            collective_id=0, has_side_effects=True, vmem_limit_bytes=40 << 20
        ),
        name="move",
    )(*(pltpu.with_memory_space_constraint(a, pltpu.HBM) for a in (spectra, freq_idx, pairing)))


def finish_kernel(scale, part, left, done, out, rest, sems, rest_sems):
    ahead, last = done.shape[1], rest.shape[1]
    copies = []
    for half in range(2):
        for r in range(ahead):
            copies.append(pltpu.make_async_copy(done.at[half, r], out.at[half, r], sems.at[half, r]))
            copies[-1].start()
    groups = part.shape[1] // 2
    for r in range(0, last, 2):
        for piece in range(PIECES):
            def multiply(q, carry, r=r):
                for b in range(2):
                    products(scale, left, part, rest, (ahead + r) // 2, q, b, r)
                return carry

            size = groups // PIECES
            lax.fori_loop(piece * size, (piece + 1) * size, multiply, 0)
            bins = pl.ds(piece * size * 2, size * 2)
            for half in range(2):
                copies.append(
                    pltpu.make_async_copy(
                        rest.at[half, pl.ds(r, 2), bins],
                        out.at[half, pl.ds(ahead + r, 2), bins],
                        rest_sems.at[r // 2, half, piece],
                    )
                )
                copies[-1].start()
    for copy in copies:
        copy.wait()


def finish(scale, part, left, done):
    rounds = 2 * part.shape[0]
    _, ahead, bins, channels, _ = done.shape
    return pl.pallas_call(
        functools.partial(finish_kernel, scale),
        out_shape=jax.ShapeDtypeStruct((2, rounds, bins, channels, channels), done.dtype),
        in_specs=[pl.BlockSpec(memory_space=pltpu.VMEM)] * 3,
        out_specs=pl.BlockSpec(memory_space=pltpu.HBM),
        scratch_shapes=[
            pltpu.VMEM((2, rounds - ahead, bins, channels, channels), done.dtype),
            pltpu.SemaphoreType.DMA((2, ahead)),
            pltpu.SemaphoreType.DMA(((rounds - ahead) // 2, 2, PIECES)),
        ],
        compiler_params=pltpu.CompilerParams(vmem_limit_bytes=16 << 20),
        name="finish",
    )(part, left, done)


def body(spectra, freq_idx, pairing):
    scale = 1.0 / math.sqrt(spectra.shape[2] * lax.axis_size("win"))
    part, left, done = move(spectra, freq_idx, pairing)
    return finish(scale, part, left, done)


def solution(mesh):
    return jax.shard_map(
        body,
        mesh=mesh,
        in_specs=(P(None, None, "win", "chan"), P(), P()),
        out_specs=P(None, None, "win", "chan", None),
        check_vma=False,
    )
```

```python
import functools
import math

import jax
import jax.numpy as jnp
from jax import lax
from jax.experimental import pallas as pl
from jax.experimental.pallas import tpu as pltpu
from jax.sharding import PartitionSpec as P

MESH = pl.DeviceIdType.MESH


def block_of(x, zh, y, c):
    return ((x * 2 + zh) * 4 + y) * 2 + c


def place(x, zh, w, y, c):
    return {"chan": block_of(x, zh, y, c), "win": w}


AHEAD = 4
PIECES = 4
BINS = 4
CUTS = ((0, 1), (1, 3))


def move_kernel(
    spectra, freq_in, pairing_in, part, left, done,
    whole_real, whole_imag, freq, pairing, sel, own,
    held_a0, held_a1, held_b0, held_b1, held_c0, held_c1, held_d0, held_d1,
    half_c0, half_c1, half_d0, half_d1,
    stage_a0, stage_a1, stage_b0, stage_b1, stage_c0, stage_c1, stage_d0, stage_d1,
    load_sem, spread_send, spread_recv, ring_send, ring_recv, far_send, far_recv, near_send, near_recv,
    mate_send, mate_recv, own_send, own_recv, part_send, part_recv,
):
    held = ((held_a0, held_a1), (held_b0, held_b1), (held_c0, held_c1), (held_d0, held_d1))
    half = ((half_c0, half_c1), (half_d0, half_d1))
    stage = ((stage_a0, stage_a1), (stage_b0, stage_b1), (stage_c0, stage_c1), (stage_d0, stage_d1))
    chan = lax.axis_index("chan")
    w = lax.axis_index("win")
    c = chan % 2
    y = (chan // 2) % 4
    zh = (chan // 8) % 2
    x = chan // 16
    pairs = pairing.shape[0] // 2

    loads = [
        pltpu.make_async_copy(src, dst, load_sem.at[n])
        for n, (src, dst) in enumerate(
            ((freq_in, freq), (pairing_in, pairing), (spectra.at[0], whole_real), (spectra.at[1], whole_imag))
        )
    ]
    for load in loads:
        load.start()

    barrier = pltpu.get_barrier_semaphore()

    def greet(dx, dz, dy, dc):
        z = (zh * 2 + w + dz) % 4
        pl.semaphore_signal(
            barrier, inc=1, device_id=place((x + dx) % 4, z // 2, z % 2, (y + dy) % 4, (c + dc) % 2),
            device_id_type=MESH,
        )

    def greet_plane(o, carry):
        dc, one, two = o % 2, (o // 2) % 4, o // 8
        greet(0, one, two, dc)

        @pl.when(two > 0)
        def _():
            greet(two, one, 0, dc)

        @pl.when((one > 0) & (two > 0))
        def _():
            greet(one, 0, two, dc)

        return carry

    lax.fori_loop(1, 32, greet_plane, 0)
    loads[0].wait()
    for half_at, whole in enumerate((whole_real, whole_imag)):
        loads[2 + half_at].wait()

        def pick(k, carry, half_at=half_at, whole=whole):
            sel[half_at, k // 32, k % 32] = whole[freq[k]]
            return carry

        lax.fori_loop(0, 64, pick, 0, unroll=16)
    loads[1].wait()
    pl.semaphore_wait(barrier, 31 + 24 + 18)

    def send(src, dst, ssem, rsem, target):
        pltpu.make_async_remote_copy(
            src_ref=src, dst_ref=dst, send_sem=ssem, recv_sem=rsem, device_id=target, device_id_type=MESH
        ).start()

    def arrived(ref, sem):
        pltpu.make_async_copy(ref, ref, sem).wait()

    def bins_of(n, t, group):
        start, size = CUTS[t]
        return pl.ds((2 * n + group) * BINS + start, size)

    def chunk_of(n, zh2, x2, y2, core):
        major = y2 if n in (0, 2) else x2
        minor = (zh2, zh2, pair_of(x2, core), pair_of(y2, core))[n]
        return major % 2, major // 2, minor

    def pick_by(core, zero, one):
        return (1 - core) * zero + core * one

    def across(at, bit, core):
        return at + bit * pick_by(core, 3 - 2 * at, 1 - 2 * (at % 2))

    def pair_of(at, core):
        return pick_by(core, at // 2, ((at + 1) // 2) % 2)

    def side_of(at, core):
        return pair_of(at, 1 - core)

    def index_of(n, p):
        x2, zh2, y2, c2 = p // 16, (p // 8) % 2, (p // 2) % 4, p % 2
        if n == 0:
            return p
        if n == 1:
            return y2 * 16 + x2 * 4 + zh2 * 2 + c2
        if n == 2:
            return side_of(x2, c) * 32 + zh2 * 16 + pair_of(x2, c) * 8 + y2 * 2 + c2
        return side_of(y2, c) * 32 + zh2 * 16 + pair_of(y2, c) * 8 + x2 * 2 + c2

    mine_half = (pair_of(x, w) * 8 + y * 2 + c, pair_of(y, w) * 8 + x * 2 + c)

    def source(n, t, zh2, w2, x2, y2):
        group, part_half, windows = chunk_of(n, zh2, x2, y2, w)
        return sel.at[part_half, w2 if n < 2 else slice(None), bins_of(n, t, group), windows]

    def landing(n, t):
        return held[n][t].at[index_of(n, chan)] if n < 2 else half[n - 2][t].at[:, mine_half[n - 2]]

    def spread_to(n, o):
        if n == 0:
            return (zh + o) % 2, (w + o // 2) % 2, x, (y + o // 4) % 4
        if n == 1:
            return (zh + o) % 2, (w + o // 2) % 2, (x + o // 4) % 4, y
        if n == 2:
            return zh, w, across(x, o % 2, w), (y + o // 2) % 4
        return zh, w, (x + o // 2) % 4, across(y, o % 2, w)

    def spread_one(n, t, o):
        zh2, w2, x2, y2 = spread_to(n, o)
        send(
            source(n, t, zh2, w2, x2, y2), landing(n, t),
            spread_send.at[t, n], spread_recv.at[t, n], place(x2, zh2, w2, y2, w),
        )

    for t in range(2):
        def spread(i, carry, t=t):
            spread_one(0, t, (i * 10) % 16)
            spread_one(1, t, (i * 14) % 16)
            spread_one(0, t, (i * 10 + 5) % 16)
            spread_one(1, t, (i * 14 + 7) % 16)
            return carry

        def spread_deep(i, carry, t=t):
            spread_one(2, t, (i * 3) % 8)
            spread_one(3, t, (i * 5) % 8)
            return carry

        lax.fori_loop(1, 8, spread_deep, 0)
        lax.fori_loop(1, 8, spread, 0)
        spread_one(0, t, 5)
        spread_one(1, t, 7)

        @pl.when(c == w)
        def _():
            for n in range(4):
                pltpu.make_async_copy(source(n, t, zh, w, x, y), landing(n, t), spread_recv.at[t, n]).start()

        @pl.when(c != w)
        def _():
            for n in range(4):
                spread_one(n, t, 0)

    def line(n, d):
        return place((x + d) % 4, zh, w, y, c) if n == 0 else place(x, zh, w, (y + d) % 4, c)

    sides = (side_of(x, c), side_of(y, c))
    mates = (place(across(x, 1, 1 - c), zh, w, y, c), place(x, zh, w, across(y, 1, 1 - c), c))

    def pass_on(t):
        @pl.when(c == w)
        def _():
            for n in range(2):
                arrived(half[n][t], spread_recv.at[t, 2 + n])
                block = held[2 + n][t].at[pl.ds(sides[n] * 32 + zh * 16, 16)]
                for k, (dzh, dw) in enumerate(((1, 0), (0, 1), (1, 1))):
                    zh2, w2 = (zh + dzh) % 2, (w + dw) % 2
                    send(half[n][t].at[w2], block, near_send.at[t, n, k], near_recv.at[t, n], place(x, zh2, w2, y, c))
                pltpu.make_async_copy(half[n][t].at[w], block, near_recv.at[t, n]).start()

        for n, at in enumerate((x, y)):
            block = held[n][t].at[pl.ds(at * 16, 16)]
            arrived(block, spread_recv.at[t, n])
            for k, d in enumerate((1, 3)):
                send(block, block, ring_send.at[t, n], ring_recv.at[t, n, k], line(n, d))

    def pass_far(t):
        for n, at in enumerate((x, y)):
            for k, d in enumerate((3, 1)):
                arrived(held[n][t].at[pl.ds(((at + d) % 4) * 16, 16)], ring_recv.at[t, n, k])
                block = held[n][t].at[pl.ds(((at + d) % 4) * 16 + 8 * k, 8)]
                send(block, block, far_send.at[t, n], far_recv.at[t, n], line(n, 4 - d))
        for n in range(2):
            block = held[2 + n][t].at[pl.ds(sides[n] * 32, 32)]
            arrived(block, near_recv.at[t, n])
            send(block, block, mate_send.at[t, n], mate_recv.at[t, n], mates[n])

    def pass_end(t):
        for n in range(2):
            arrived(held[n][t].at[pl.ds(0, 16)], far_recv.at[t, n])
            arrived(held[2 + n][t].at[pl.ds(0, 32)], mate_recv.at[t, n])

    def fill(n, t, slot, pair, b):
        group, part_half, windows = chunk_of(n, zh, x, y, c)
        bins = bins_of(n, t, group)
        if t == 0:
            for r in range(2 * pairs):
                stage[n][t][slot, r // 2, :, r % 2] = held[n][t][index_of(n, pairing[r, b])]
            return part.at[:, bins, part_half, :, c, windows]
        for k in range(2):
            stage[n][t][slot, :, k] = held[n][t][index_of(n, pairing[2 * pair + k, b])]
        return part.at[pair, bins, part_half, :, c, windows]

    def due(t, pair):
        return part_recv.at[pairs if t == 0 else pair]

    def give_one(n, t, j):
        pair, o = j // 15, ((j % 15 + 1) * (5, 11, 3, 7)[n]) % 16
        c2 = (c + o // 8) % 2
        zh2, x2, y2 = (
            ((zh + o) % 2, x, (y + o // 2) % 4),
            ((zh + o // 4) % 2, (x + o) % 4, y),
            (zh, across(x, (o // 4) % 2, c), (y + o) % 4),
            (zh, (x + o // 2) % 4, across(y, o % 2, c)),
        )[n]
        dst = fill(n, t, j, pair, block_of(x2, zh2, y2, c2))
        send(stage[n][t].at[j], dst, part_send.at[t, n], due(t, pair), place(x2, zh2, w, y2, c2))

    def give(t, begin, end):
        def step(i, carry):
            each = 1 if t == 0 else pairs
            for k in range(each):
                for n in (0, 2, 1, 3):
                    give_one(n, t, each * i + k)
            return carry

        lax.fori_loop(begin, end, step, 0)

    def keep(t):
        def step(pair, carry):
            for n in range(4):
                slot = copies[t] + pair
                dst = fill(n, t, slot, pair, chan)
                pltpu.make_async_copy(stage[n][t].at[slot], dst, due(t, pair)).start()
            return carry

        lax.fori_loop(0, copies[t] // 15, step, 0)

    copies = (15, 15 * pairs)
    turns = 15
    pass_on(0)
    pass_far(0)
    pass_on(1)
    pass_end(0)
    keep(0)
    give(0, 0, turns // 5)
    pass_far(1)
    send(sel.at[:, 1 - w], own.at[:, :, w], own_send, own_recv, place(x, zh, 1 - w, y, c))
    pltpu.make_async_copy(sel.at[:, w], own.at[:, :, w], own_recv).start()
    give(0, turns // 5, turns)
    pass_end(1)
    keep(1)
    give(1, 0, turns)

    arrived(sel, own_recv)

    def turn(k, carry):
        real = own[0, k].reshape(-1, own.shape[-1])
        imag = own[1, k].reshape(-1, own.shape[-1])
        channels = real.shape[1]
        left[k, :channels] = jnp.concatenate([real, imag], 0).T
        left[k, channels:] = jnp.concatenate([imag, -real], 0).T
        return carry

    lax.fori_loop(0, left.shape[0], turn, 0)
    scale = 1.0 / math.sqrt(own.shape[2] * own.shape[3] * own.shape[4])
    early = part.shape[1] * CUTS[0][1] // BINS
    arrived(part.at[0, pl.ds(0, early * pairs)], part_recv.at[pairs])
    for pair in range(pairs):
        arrived(part.at[pair, pl.ds(early, part.shape[1] - early)], part_recv.at[pair])
        if 2 * pair < AHEAD:
            def multiply(q, carry, pair=pair):
                for b in range(2):
                    products(scale, left, part, done, pair, q, b, 2 * pair)
                return carry

            lax.fori_loop(0, part.shape[1] // 2, multiply, 0)

    for t in range(2):
        def gone(missing, t=t):
            for n in range(2):
                arrived(held[n][t].at[pl.ds(0, 16 - missing)], spread_send.at[t, n])
                arrived(half[n][t].at[:, pl.ds(0, 8 - missing)], spread_send.at[t, 2 + n])

        @pl.when(c == w)
        def _():
            gone(1)
            for n in range(2):
                for k in range(3):
                    arrived(held[2 + n][t].at[pl.ds(0, 16)], near_send.at[t, n, k])

        @pl.when(c != w)
        def _():
            gone(0)

        for n in range(2):
            arrived(held[n][t].at[pl.ds(0, 32)], ring_send.at[t, n])
            arrived(held[n][t].at[pl.ds(0, 16)], far_send.at[t, n])
            arrived(held[2 + n][t].at[pl.ds(0, 32)], mate_send.at[t, n])
        for n in range(4):
            arrived(stage[n][t].at[pl.ds(0, copies[t])], part_send.at[t, n])
    arrived(sel.at[:, 0], own_send)


def products(scale, left, part, out, pair, q, b, r):
    channels = left.shape[2]
    right = jnp.concatenate(
        [
            jnp.concatenate([part[pair, 2 * q + b, half, n].reshape(-1, channels) for half in range(2)], 0)
            for n in range(2)
        ],
        1,
    )
    product = jnp.dot(left[2 * q + b], right, preferred_element_type=jnp.float32) * scale
    product = product.astype(out.dtype)
    for half in range(2):
        for n in range(2):
            out[half, r + n, 2 * q + b] = product[
                half * channels : (half + 1) * channels, n * channels : (n + 1) * channels
            ]


def move(spectra, freq_idx, pairing):
    _, nbins, width, channels = spectra.shape
    rounds = pairing.shape[0]
    kind = spectra.dtype
    tile = (width // 2, channels)
    spectra = spectra.reshape((2, nbins, 2) + tile)
    sizes = [n for _, n in CUTS]
    return pl.pallas_call(
        move_kernel,
        out_shape=(
            pltpu.VMEM((rounds // 2, 32, 2, 2, 2, 2) + tile, kind),
            pltpu.VMEM((32, 2 * channels, channels), kind),
            pltpu.VMEM((2, AHEAD, 32, channels, channels), kind),
        ),
        in_specs=[pl.BlockSpec(memory_space=pltpu.HBM)] * 3,
        out_specs=(pl.BlockSpec(memory_space=pltpu.VMEM),) * 3,
        scratch_shapes=[
            pltpu.VMEM(spectra.shape[1:], kind),
            pltpu.VMEM(spectra.shape[1:], kind),
            pltpu.SMEM(freq_idx.shape, freq_idx.dtype),
            pltpu.SMEM(pairing.shape, pairing.dtype),
            pltpu.VMEM((2, 2, 32, 2) + tile, kind),
            pltpu.VMEM((2, 32, 2, 2) + tile, kind),
            *[pltpu.VMEM((64, n) + tile, kind) for _ in range(4) for n in sizes],
            *[pltpu.VMEM((2, 16, n) + tile, kind) for _ in range(2) for n in sizes],
            *[
                pltpu.VMEM(shape + tile, kind)
                for _ in range(4)
                for shape in ((16, rounds // 2, sizes[0], 2), (8 * rounds, sizes[1], 2))
            ],
            pltpu.SemaphoreType.DMA((4,)),
            pltpu.SemaphoreType.DMA((2, 4)),
            pltpu.SemaphoreType.DMA((2, 4)),
            pltpu.SemaphoreType.DMA((2, 2)),
            pltpu.SemaphoreType.DMA((2, 2, 2)),
            pltpu.SemaphoreType.DMA((2, 2)),
            pltpu.SemaphoreType.DMA((2, 2)),
            pltpu.SemaphoreType.DMA((2, 2, 3)),
            pltpu.SemaphoreType.DMA((2, 2)),
            pltpu.SemaphoreType.DMA((2, 2)),
            pltpu.SemaphoreType.DMA((2, 2)),
            pltpu.SemaphoreType.DMA,
            pltpu.SemaphoreType.DMA,
            pltpu.SemaphoreType.DMA((2, 4)),
            pltpu.SemaphoreType.DMA((rounds // 2 + 1,)),
        ],
        compiler_params=pltpu.CompilerParams(
            collective_id=0, has_side_effects=True, vmem_limit_bytes=40 << 20
        ),
        name="move",
    )(*(pltpu.with_memory_space_constraint(a, pltpu.HBM) for a in (spectra, freq_idx, pairing)))


def finish_kernel(scale, part, left, done, out, rest, sems, rest_sems):
    ahead, last = done.shape[1], rest.shape[1]
    copies = []
    for half in range(2):
        for r in range(ahead):
            copies.append(pltpu.make_async_copy(done.at[half, r], out.at[half, r], sems.at[half, r]))
            copies[-1].start()
    groups = part.shape[1] // 2
    for r in range(0, last, 2):
        for piece in range(PIECES):
            def multiply(q, carry, r=r):
                for b in range(2):
                    products(scale, left, part, rest, (ahead + r) // 2, q, b, r)
                return carry

            size = groups // PIECES
            lax.fori_loop(piece * size, (piece + 1) * size, multiply, 0)
            bins = pl.ds(piece * size * 2, size * 2)
            for half in range(2):
                copies.append(
                    pltpu.make_async_copy(
                        rest.at[half, pl.ds(r, 2), bins],
                        out.at[half, pl.ds(ahead + r, 2), bins],
                        rest_sems.at[r // 2, half, piece],
                    )
                )
                copies[-1].start()
    for copy in copies:
        copy.wait()


def finish(scale, part, left, done):
    rounds = 2 * part.shape[0]
    _, ahead, bins, channels, _ = done.shape
    return pl.pallas_call(
        functools.partial(finish_kernel, scale),
        out_shape=jax.ShapeDtypeStruct((2, rounds, bins, channels, channels), done.dtype),
        in_specs=[pl.BlockSpec(memory_space=pltpu.VMEM)] * 3,
        out_specs=pl.BlockSpec(memory_space=pltpu.HBM),
        scratch_shapes=[
            pltpu.VMEM((2, rounds - ahead, bins, channels, channels), done.dtype),
            pltpu.SemaphoreType.DMA((2, ahead)),
            pltpu.SemaphoreType.DMA(((rounds - ahead) // 2, 2, PIECES)),
        ],
        compiler_params=pltpu.CompilerParams(vmem_limit_bytes=16 << 20),
        name="finish",
    )(part, left, done)


def body(spectra, freq_idx, pairing):
    scale = 1.0 / math.sqrt(spectra.shape[2] * lax.axis_size("win"))
    part, left, done = move(spectra, freq_idx, pairing)
    return finish(scale, part, left, done)


def solution(mesh):
    return jax.shard_map(
        body,
        mesh=mesh,
        in_specs=(P(None, None, "win", "chan"), P(), P()),
        out_specs=P(None, None, "win", "chan", None),
        check_vma=False,
    )
```
